32 devices in a mesh: groups: 2 (over y), latent: 4 (over z), dp: 2 (over x), sub: 2 (over core).
Axes of the slice: x: 2, y: 2, z: 4, core: 2. Of those that a mesh axis runs over, the one named last changes fastest.
Arguments:
- inputs: bfloat16 [448, 4096], P(('groups', 'latent'), ('dp', 'sub')), parts along dimension 0, may hold values from -6 to 6
- dec_bias: float32 [8192], P(('groups', 'dp', 'sub')), parts along dimension 0, may hold values from -3 to 3
- enc_master: float32 [1664, 4096], P(('groups', 'latent'), ('dp', 'sub')), parts along dimension 0, may hold values from -0.09375 to 0.09375
- enc_bias: float32 [1664], P(('groups', 'latent')), parts along dimension 0, may hold values from -3 to 3
- dec_master: float32 [1664, 4096], P(('groups', 'latent'), ('dp', 'sub')), parts along dimension 0, may hold values from -0.25 to 0.25
- enc_m: float32 [1664, 4096], P(('groups', 'latent'), ('dp', 'sub')), parts along dimension 0, may hold values from -0.0006 to 0.0006
- enc_v: float32 [1664, 4096], P(('groups', 'latent'), ('dp', 'sub')), parts along dimension 0, may hold values from 1e-09 to 1e-07
- dec_m: float32 [1664, 4096], P(('groups', 'latent'), ('dp', 'sub')), parts along dimension 0, may hold values from -0.0006 to 0.0006
- dec_v: float32 [1664, 4096], P(('groups', 'latent'), ('dp', 'sub')), parts along dimension 0, may hold values from 1e-09 to 1e-07
- bias_m: float32 [1664], P(('groups', 'latent')), parts along dimension 0, may hold values from -0.0006 to 0.0006
- bias_v: float32 [1664], P(('groups', 'latent')), parts along dimension 0, may hold values from 1e-09 to 1e-07
Outputs:
- enc_new: float32 [1664, 4096], P(('groups', 'latent'), ('dp', 'sub')), parts along dimension 0
- bias_new: float32 [1664], P(('groups', 'latent')), parts along dimension 0
- dec_new: float32 [1664, 4096], P(('groups', 'latent'), ('dp', 'sub')), parts along dimension 0
- enc_m_new: float32 [1664, 4096], P(('groups', 'latent'), ('dp', 'sub')), parts along dimension 0
- enc_v_new: float32 [1664, 4096], P(('groups', 'latent'), ('dp', 'sub')), parts along dimension 0
- dec_m_new: float32 [1664, 4096], P(('groups', 'latent'), ('dp', 'sub')), parts along dimension 0
- dec_v_new: float32 [1664, 4096], P(('groups', 'latent'), ('dp', 'sub')), parts along dimension 0
- bias_m_new: float32 [1664], P(('groups', 'latent')), parts along dimension 0
- bias_v_new: float32 [1664], P(('groups', 'latent')), parts along dimension 0
- loss: float32 [2], P('groups'), parts along dimension 0
The draws below stay inside these ranges and needn't reach their ends.
There are 2 independent parts, one for each index of `groups`. The reference program is written for one: setup_inputs(seed, part) draws one part's arguments, and reference() takes and returns one part's arrays. A program takes and returns all parts, laid end to end along the dimension named above; each array names one. Nothing has to cross between parts.
All inputs are finite; a program needn't handle non-finite values.
Results may differ from the reference program's by a relative error of at most 0.0049.
Values may be sent and summed in bfloat16 or wider, within the bound.
A program may use at most 64 MiB of HBM per device.

```python
import math
import jax
import jax.numpy as jnp
from jax import lax

D = 4096
LAT_DEV = 208
LATENTS = 832
TOKENS = 224
FEAT_DEV = 1024


def shared_direction(key):
    blocks = D // FEAT_DEV
    levels = jnp.exp(jax.random.uniform(jax.random.fold_in(key, 501), (blocks,), jnp.float32, jnp.log(0.4), jnp.log(2.0)))
    vector = jax.random.normal(jax.random.fold_in(key, 502), (D,), jnp.float32)
    return vector * jnp.repeat(levels, FEAT_DEV)


def draw_inputs(key, part):
    direction = shared_direction(key)
    key = jax.random.fold_in(key, 11)
    noise_key, weight_key = jax.random.split(key)
    noise = jax.random.normal(noise_key, (TOKENS, D), jnp.float32)
    token_weight = 0.9 * jax.random.normal(weight_key, (TOKENS, 1), jnp.float32)
    return jnp.clip(noise + token_weight * direction, -6.0, 6.0).astype(jnp.bfloat16)


def draw_dec_master(key, part):
    direction = shared_direction(key)
    key = jax.random.fold_in(key, 12)
    keys = jax.random.split(key, 4)
    blocks = LATENTS // LAT_DEV
    block_align = jnp.exp(jax.random.uniform(keys[0], (blocks,), jnp.float32, jnp.log(0.005), jnp.log(0.04)))
    latent_sign = jax.random.normal(keys[1], (LATENTS, 1), jnp.float32)
    noise = jax.random.truncated_normal(keys[2], -4.0, 4.0, (LATENTS, D), jnp.float32)
    order = jax.random.permutation(keys[3], blocks)
    row_block = jnp.arange(LATENTS) // LAT_DEV
    col_block = jnp.arange(D) // (D // blocks)
    boost = jnp.where(order[row_block][:, None] == col_block[None, :], 3.0, 1.0)
    align = jnp.repeat(block_align, LAT_DEV)[:, None] * latent_sign
    values = (noise * boost + align * direction[None, :]) * float(D) ** (-0.5)
    return jnp.clip(values, -0.25, 0.25)


def block_scale(key, shape, pieces, least, largest):
    loudness = 1.0
    for dim, blocks in pieces:
        heights = jax.random.uniform(jax.random.fold_in(jax.random.fold_in(key, 6), dim), (blocks,), jnp.float32, least / len(pieces), largest / len(pieces))
        loudness = loudness * jnp.repeat(jnp.exp(heights), shape[dim] // blocks).reshape((-1,) + (1,) * (len(shape) - 1 - dim))
    return loudness


def gaussian(rng, dims, scale, most, shards=(), dtype=jnp.bfloat16):
    factor_of = block_scale(rng, dims, shards, -0.22, 0.18) if shards else 1.0
    drawn = jax.random.normal(rng, dims, jnp.float32) * scale * factor_of
    return jnp.minimum(jnp.maximum(drawn, -most), most).astype(dtype)


def setup_inputs(seed: int = 0, part: int = 0) -> dict:
    splits = jax.random.split(jax.random.key(seed), 12)
    own_keys = jax.random.split(jax.random.fold_in(splits[11], part), 12)
    inputs = draw_inputs(jax.random.fold_in(jax.random.fold_in(splits[11], part), 71), part)
    dec_bias = gaussian(own_keys[1], (D,), 0.3, 3.0, ((0, 4),), jnp.float32)
    enc_master = gaussian(own_keys[2], (LATENTS, D), D ** -0.5, 0.09375, ((0, 4), (1, 4)), jnp.float32)
    enc_bias = gaussian(own_keys[3], (LATENTS,), 0.3, 3.0, ((0, 4),), jnp.float32)
    dec_master = draw_dec_master(jax.random.fold_in(jax.random.fold_in(splits[11], part), 71), part)
    enc_m = gaussian(own_keys[5], (LATENTS, D), 0.0001, 0.0006, ((0, 4), (1, 4)), jnp.float32)
    enc_v = jnp.clip(jnp.exp(math.log(1.0000000116860974e-07) - 4.6051702 * jax.random.uniform(own_keys[6], (LATENTS, D), jnp.float32) ** block_scale(own_keys[6], (LATENTS, D), ((0, 4), (1, 4)), -0.2, 0.2)), 9.999999717180685e-10, 1.0000000116860974e-07)
    dec_m = gaussian(own_keys[7], (LATENTS, D), 0.0001, 0.0006, ((0, 4), (1, 4)), jnp.float32)
    dec_v = jnp.clip(jnp.exp(math.log(1.0000000116860974e-07) - 4.6051702 * jax.random.uniform(own_keys[8], (LATENTS, D), jnp.float32) ** block_scale(own_keys[8], (LATENTS, D), ((0, 4), (1, 4)), -0.2, 0.2)), 9.999999717180685e-10, 1.0000000116860974e-07)
    bias_m = gaussian(own_keys[9], (LATENTS,), 0.0001, 0.0006, ((0, 4),), jnp.float32)
    bias_v = jnp.clip(jnp.exp(math.log(1.0000000116860974e-07) - 4.6051702 * jax.random.uniform(own_keys[10], (LATENTS,), jnp.float32) ** block_scale(own_keys[10], (LATENTS,), ((0, 4),), -0.2, 0.2)), 9.999999717180685e-10, 1.0000000116860974e-07)
    return {"inputs": inputs, "dec_bias": dec_bias, "enc_master": enc_master, "enc_bias": enc_bias, "dec_master": dec_master, "enc_m": enc_m, "enc_v": enc_v, "dec_m": dec_m, "dec_v": dec_v, "bias_m": bias_m, "bias_v": bias_v}


sparsity_coef = 5.0
clip_norm = 1.0
learn_rate = 0.01
beta_one = 0.9
beta_two = 0.999
adam_step = 100

def adam_update(master, moment_one, moment_two, gradient):
    new_one = beta_one * moment_one + (1.0 - beta_one) * gradient
    new_two = beta_two * moment_two + (1.0 - beta_two) * gradient * gradient
    fix_one = 1.0 - beta_one ** adam_step
    fix_two = 1.0 - beta_two ** adam_step
    updated = master - learn_rate * (new_one / fix_one) / (jnp.sqrt(new_two / fix_two) + 1e-08)
    return (updated, new_one, new_two)

def reference(inputs, dec_bias, enc_master, enc_bias, dec_master, enc_m, enc_v, dec_m, dec_v, bias_m, bias_v):
    centered = (inputs.astype(jnp.float32) - dec_bias).astype(jnp.bfloat16)
    enc_copy = enc_master.astype(jnp.bfloat16)
    dec_copy = dec_master.astype(jnp.bfloat16)
    contract = (((1,), (1,)), ((), ()))
    preact = lax.dot_general(centered, enc_copy, contract, preferred_element_type=jnp.float32) + enc_bias
    active = jnp.maximum(preact, 0.0)
    active_b = active.astype(jnp.bfloat16)
    recon = jnp.dot(active_b, dec_copy, preferred_element_type=jnp.float32)
    residual = recon + dec_bias - inputs.astype(jnp.float32)
    dec_norms = jnp.sqrt(lax.optimization_barrier(jnp.sum(dec_master * dec_master, axis=1)) + 1e-06)
    loss = (jnp.sum(residual * residual) + sparsity_coef * jnp.sum(active * dec_norms)) / TOKENS
    out_grad = (residual * (2.0 / TOKENS)).astype(jnp.bfloat16)
    first_dims = (((0,), (0,)), ((), ()))
    dec_grad = lax.dot_general(active_b, out_grad, first_dims, preferred_element_type=jnp.float32)
    dec_grad = dec_grad + sparsity_coef / TOKENS * lax.optimization_barrier(jnp.sum(active, axis=0))[:, None] * dec_master / dec_norms[:, None]
    back = lax.dot_general(out_grad, dec_copy, contract, preferred_element_type=jnp.float32) + sparsity_coef / TOKENS * dec_norms
    pre_grad = jnp.where(preact > 0.0, back, 0.0)
    pre_grad_b = pre_grad.astype(jnp.bfloat16)
    enc_grad = lax.dot_general(pre_grad_b, centered, first_dims, preferred_element_type=jnp.float32)
    bias_grad = lax.optimization_barrier(jnp.sum(pre_grad, axis=0))
    grad_square = jnp.sum(enc_grad * enc_grad) + jnp.sum(dec_grad * dec_grad) + jnp.sum(bias_grad * bias_grad)
    clip_scale = jnp.minimum(1.0, clip_norm / jnp.sqrt(grad_square + 1e-12))
    enc_new, enc_m_new, enc_v_new = adam_update(enc_master, enc_m, enc_v, clip_scale * enc_grad)
    bias_new, bias_m_new, bias_v_new = adam_update(enc_bias, bias_m, bias_v, clip_scale * bias_grad)
    dec_new, dec_m_new, dec_v_new = adam_update(dec_master, dec_m, dec_v, clip_scale * dec_grad)
    return (enc_new, bias_new, dec_new, enc_m_new, enc_v_new, dec_m_new, dec_v_new, bias_m_new, bias_v_new, jnp.reshape(loss, (1,)))
```

```python
import functools

import jax
import jax.numpy as jnp
from jax import lax
from jax.experimental import pallas as pl
from jax.experimental.pallas import tpu as pltpu
from jax.sharding import PartitionSpec as P

sparsity_coef = 5.0
clip_norm = 1.0
learn_rate = 0.01
beta_one = 0.9
beta_two = 0.999
adam_step = 100

MESH = pl.DeviceIdType.MESH
F32 = jnp.float32
BF16 = jnp.bfloat16
NT = (((1,), (1,)), ((), ()))
TN = (((0,), (0,)), ((), ()))


def adam_update(master, moment_one, moment_two, gradient):
    new_one = beta_one * moment_one + (1.0 - beta_one) * gradient
    new_two = beta_two * moment_two + (1.0 - beta_two) * gradient * gradient
    fix_one = 1.0 - beta_one**adam_step
    fix_two = 1.0 - beta_two**adam_step
    updated = master - learn_rate * (new_one / fix_one) / (jnp.sqrt(new_two / fix_two) + 1e-08)
    return (updated, new_one, new_two)


def when(cond):
    if isinstance(cond, bool):
        return (lambda f: f()) if cond else (lambda f: None)
    return pl.when(cond)


def steps(low, high, body, unroll):
    if unroll:
        for j in range(low, high):
            body(j)
    else:
        lax.fori_loop(low, high, lambda j, _: (body(j), 0)[1], 0)


def kernel(
    Z, X, C, rows, x_ref, bias_ref, enc_bias_ref, enc_hbm, dec_hbm,
    enc_grad_ref, dec_grad_ref, bias_grad_ref, scalar_ref,
    enc_f, dec_f, enc_b, dec_b,
    cent_tx, cent_rx, cent, part_tx, part_rx, norm_tx, norm_rx, norm_row, act, recon_own,
    recon_tx, recon_rx, grad_tx, grad_rx, grad, back_tx, back_rx, pre, loss_acc, square_acc,
    one_rx, two_tx, two_rx,
    load_sem, cent_s, cent_r, part_s, part_r, norm_s, norm_r, act_s, act_r,
    recon_s, recon_r, grad_s, grad_r, back_s, back_r, pre_s, pre_r, one_s, one_r, two_s, two_r,
):
    n = X * C
    B = Z // n
    unroll = Z <= 4
    pad = cent.shape[1]
    width = cent.shape[2]
    half = width // 2
    lat = enc_f.shape[0]
    tokens = Z * rows
    z = lax.axis_index("latent")
    f = lax.axis_index("dp") * C + lax.axis_index("sub")

    def zdev(k):
        return {"latent": lax.rem(z + k, Z)}

    def fdev(q):
        return {"dp": lax.div(q, C), "sub": lax.rem(q, C)}

    def fpeer(k):
        return lax.rem(f + k, n)

    def remote(src, dst, s, r, dev):
        return pltpu.make_async_remote_copy(
            src_ref=src, dst_ref=dst, send_sem=s, recv_sem=r, device_id=dev, device_id_type=MESH
        )

    load_enc = pltpu.make_async_copy(enc_hbm, enc_f, load_sem.at[0])
    load_dec = pltpu.make_async_copy(dec_hbm, dec_f, load_sem.at[1])
    load_enc.start()
    load_dec.start()

    barrier = pltpu.get_barrier_semaphore()
    for k in range(1, Z):
        pl.semaphore_signal(barrier, inc=1, device_id=zdev(k), device_id_type=MESH)
    for k in range(1, n):
        pl.semaphore_signal(barrier, inc=1, device_id=fdev(fpeer(k)), device_id_type=MESH)

    def pack(ref, value):
        ref[...] = jnp.concatenate([value[:, :half], value[:, half:]], axis=0).astype(BF16)

    def unpack(ref):
        both = ref[...].astype(F32)
        return both[:rows], both[rows:]

    def place(ref, left, right):
        ref[:rows, :half] = left.astype(BF16)
        ref[:rows, half:] = right.astype(BF16)
        ref[rows:, :] = jnp.zeros((pad - rows, width), BF16)

    x_own = x_ref[...].astype(F32)
    centered = x_own - bias_ref[...]
    pack(cent_tx, centered)
    place(cent.at[0], centered[:, :half], centered[:, half:])
    pl.semaphore_wait(barrier, Z - 1 + n - 1)

    def cent_copy(k):
        return remote(cent_tx, cent_rx.at[Z - k], cent_s.at[k], cent_r.at[Z - k], zdev(k))

    def recon_copy(j):
        return remote(recon_tx.at[j], recon_rx.at[Z - j], recon_s.at[j], recon_r.at[Z - j], zdev(j))

    def grad_copy(k):
        return remote(grad_tx, grad_rx.at[Z - k], grad_s.at[k], grad_r.at[Z - k], zdev(k))

    def norm_copy(k):
        return remote(norm_tx, norm_rx.at[f], norm_s.at[k], norm_r.at[f], fdev(fpeer(k)))

    def part_copy(tx, rx, s, r, j):
        return remote(tx.at[j], rx.at[j % B, f], s.at[j], r.at[j % B, f], fdev(j // B))

    def arrival(rx, s, r, jj, k):
        q = fpeer(k)
        return remote(rx.at[jj, q], rx.at[jj, q], s.at[0], r.at[jj, q], fdev(q))

    def share_copy(buf, s, r, j, k):
        return remote(buf.at[j], buf.at[j], s.at[j % B, k], r.at[j], fdev(fpeer(k)))

    def shared(buf, s, r, j):
        return remote(buf.at[j], buf.at[j], s.at[0, 0], r.at[j], fdev(fpeer(1)))

    for k in range(1, Z):
        cent_copy(k).start()

    load_dec.wait()
    dec = dec_f[...]
    dec_b[...] = dec.astype(BF16)
    column = jnp.sum(dec * dec, axis=1, keepdims=True)
    diag = lax.broadcasted_iota(jnp.int32, (lat, lat), 0) == lax.broadcasted_iota(
        jnp.int32, (lat, lat), 1
    )
    row = jnp.sum(jnp.where(diag, column, 0.0), axis=0, keepdims=True)
    norm_tx[...] = jnp.broadcast_to(row, norm_tx.shape)
    norm_rx[f] = jnp.broadcast_to(row, norm_tx.shape)
    for k in range(1, n):
        norm_copy(k).start()
    load_enc.wait()
    enc_b[...] = enc_f[...].astype(BF16)
    loss_acc[...] = jnp.zeros_like(loss_acc)

    def sum_parts(rx, s, r, jj):
        for k in range(1, n):
            arrival(rx, s, r, jj, k).wait_recv()
        total = rx[jj, 0]
        for q in range(1, n):
            total = total + rx[jj, q]
        return total

    def send_part(value, tx, rx, s, r, j):
        owner = j // B

        @pl.when(f == owner)
        def _():
            rx[j % B, f] = value

        @pl.when(f != owner)
        def _():
            tx[j] = value
            part_copy(tx, rx, s, r, j).start()

    def set_shared(buf, s, r, j, value):
        buf[j, :rows, :] = value.astype(BF16)
        buf[j, rows:, :] = jnp.zeros((pad - rows, lat), BF16)
        for k in range(1, n):
            share_copy(buf, s, r, j, k).start()

    def encode(j):
        @when(j > 0)
        def _():
            remote(cent_tx, cent_rx.at[j], cent_s.at[0], cent_r.at[j], zdev(1)).wait_recv()
            place(cent.at[j], *unpack(cent_rx.at[j]))

        value = lax.dot_general(cent[j], enc_b[...], NT, preferred_element_type=F32)[:rows]
        send_part(value, part_tx, part_rx, part_s, part_r, j)

    def activate(j):
        @pl.when(f == j // B)
        def _():
            total = sum_parts(part_rx, part_s, part_r, j % B)
            active = jnp.maximum(total + enc_bias_ref[...], 0.0)
            set_shared(act, act_s, act_r, j, active)
            loss_acc[:, :lat] += sparsity_coef * jnp.sum(
                active * norm_row[...], axis=0, keepdims=True
            )

    def decode(j):
        @pl.when(f != j // B)
        def _():
            shared(act, act_s, act_r, j).wait_recv()

        value = jnp.dot(act[j], dec_b[...], preferred_element_type=F32)[:rows]

        @when(j == 0)
        def _():
            recon_own[...] = value

        @when(j > 0)
        def _():
            pack(recon_tx.at[j], value)
            recon_copy(j).start()

    def finish_norms():
        for k in range(1, n):
            q = fpeer(k)
            remote(norm_tx, norm_rx.at[q], norm_s.at[0], norm_r.at[q], fdev(q)).wait_recv()
        total = norm_rx[0]
        for q in range(1, n):
            total = total + norm_rx[q]
        norm_row[...] = jnp.sqrt(total[:1] + 1e-06)

    if unroll:
        encode(0)
        finish_norms()
        activate(0)
        encode(1)
        for s in range(2, Z + 2):
            if s < Z:
                encode(s)
            if s - 1 < Z:
                activate(s - 1)
            decode(s - 2)
    else:
        finish_norms()
        steps(0, Z, encode, False)
        steps(0, Z, activate, False)
        steps(0, Z, decode, False)

    left = recon_own[:, :half]
    right = recon_own[:, half:]

    def add_rows(j, carry):
        remote(cent_tx, recon_rx.at[j], recon_s.at[0], recon_r.at[j], zdev(1)).wait_recv()
        one, two = unpack(recon_rx.at[j])
        return carry[0] + one, carry[1] + two

    if unroll:
        for j in range(1, Z):
            left, right = add_rows(j, (left, right))
    else:
        left, right = lax.fori_loop(1, Z, add_rows, (left, right))
    residual = jnp.concatenate([left, right], axis=1) + bias_ref[...] - x_own
    out_grad = residual * (2.0 / tokens)
    pack(grad_tx, out_grad)
    for k in range(1, Z):
        grad_copy(k).start()
    place(grad.at[0], out_grad[:, :half], out_grad[:, half:])
    error = jnp.sum(residual * residual, axis=0, keepdims=True)
    loss_acc[...] += error

    def back(j):
        @when(j > 0)
        def _():
            remote(grad_tx, grad_rx.at[j], grad_s.at[0], grad_r.at[j], zdev(1)).wait_recv()
            place(grad.at[j], *unpack(grad_rx.at[j]))

        value = lax.dot_general(grad[j], dec_b[...], NT, preferred_element_type=F32)[:rows]
        send_part(value, back_tx, back_rx, back_s, back_r, j)

    def through(j):
        @pl.when(f == j // B)
        def _():
            total = sum_parts(back_rx, back_s, back_r, j % B)
            total = total + (sparsity_coef / tokens) * norm_row[...]
            value = jnp.where(act[j].astype(F32)[:rows] > 0.0, total, 0.0)
            set_shared(pre, pre_s, pre_r, j, value)

    if unroll:
        back(0)
        for s in range(1, Z + 1):
            if s < Z:
                back(s)
            through(s - 1)
    else:
        steps(0, Z, back, False)
        steps(0, Z, through, False)

    act_all = act[...].reshape(Z * pad, lat)
    act_sum = jnp.sum(act_all.astype(F32), axis=0, keepdims=True)
    coef_row = (sparsity_coef / tokens) * act_sum / norm_row[...]
    coef = jnp.sum(jnp.where(diag, coef_row, 0.0), axis=1, keepdims=True)
    chunk = min(256, width)
    square_acc[...] = jnp.zeros_like(square_acc)
    for c in range(0, width, chunk):
        cols = slice(c, c + chunk)
        g = lax.dot_general(
            act_all, grad[:, :, cols].reshape(Z * pad, chunk), TN, preferred_element_type=F32
        )
        g = g + coef * dec_f[:, cols]
        dec_grad_ref[:, cols] = g
        square_acc[:, :chunk] += jnp.sum(g * g, axis=0, keepdims=True)

    def wait_pre(j):
        @pl.when(f != j // B)
        def _():
            shared(pre, pre_s, pre_r, j).wait_recv()

    steps(0, Z, wait_pre, unroll)
    pre_all = pre[...].reshape(Z * pad, lat)
    bias_grad = jnp.sum(pre_all.astype(F32), axis=0, keepdims=True)
    bias_grad_ref[...] = bias_grad
    for c in range(0, width, chunk):
        cols = slice(c, c + chunk)
        g = lax.dot_general(
            pre_all, cent[:, :, cols].reshape(Z * pad, chunk), TN, preferred_element_type=F32
        )
        enc_grad_ref[:, cols] = g
        square_acc[:, :chunk] += jnp.sum(g * g, axis=0, keepdims=True)

    first = jnp.where(f == 0, 1.0, 0.0)
    square = jnp.sum(square_acc[...], axis=1, keepdims=True) + first * jnp.sum(
        bias_grad * bias_grad, axis=1, keepdims=True
    )
    loss = jnp.sum(loss_acc[...], axis=1, keepdims=True)
    lane = lax.broadcasted_iota(jnp.int32, (8, 128), 1)
    own = jnp.where(lane == 0, loss, jnp.where(lane == 1, square, 0.0))

    one_rx[z] = own

    def one_copy(k):
        return remote(one_rx.at[z], one_rx.at[z], one_s.at[k], one_r.at[z], zdev(k))

    for k in range(1, Z):
        one_copy(k).start()
    for k in range(1, Z):
        src = lax.rem(z + k, Z)
        remote(one_rx.at[src], one_rx.at[src], one_s.at[0], one_r.at[src], zdev(k)).wait_recv()
    total = one_rx[0]
    for k in range(1, Z):
        total = total + one_rx[k]
    two_rx[f] = total

    def two_copy(k):
        return remote(two_rx.at[f], two_rx.at[f], two_s.at[k], two_r.at[f], fdev(fpeer(k)))

    for k in range(1, n):
        two_copy(k).start()
    for k in range(1, n):
        q = fpeer(k)
        remote(two_rx.at[q], two_rx.at[q], two_s.at[0], two_r.at[q], fdev(q)).wait_recv()
    total = two_rx[0]
    for q in range(1, n):
        total = total + two_rx[q]
    scale = jnp.minimum(1.0, clip_norm / jnp.sqrt(total + 1e-12))
    scalar_ref[...] = jnp.where(lane == 0, total * (1.0 / tokens), scale)

    for k in range(1, Z):
        cent_copy(k).wait_send()
        grad_copy(k).wait_send()
        one_copy(k).wait_send()
    for k in range(1, n):
        norm_copy(k).wait_send()
        two_copy(k).wait_send()

    def drain(j):
        @when(j > 0)
        def _():
            recon_copy(j).wait_send()

        @pl.when(f != j // B)
        def _():
            part_copy(part_tx, part_rx, part_s, part_r, j).wait_send()
            part_copy(back_tx, back_rx, back_s, back_r, j).wait_send()

        @pl.when(f == j // B)
        def _():
            for k in range(1, n):
                share_copy(act, act_s, act_r, j, k).wait_send()
                share_copy(pre, pre_s, pre_r, j, k).wait_send()

    steps(0, Z, drain, unroll)


def gradients(Z, X, C, inputs, dec_bias, enc_bias, enc_master, dec_master):
    rows, width = inputs.shape
    lat = enc_master.shape[0]
    n = X * C
    B = Z // n
    pad = -(-rows // 16) * 16
    dma = pltpu.SemaphoreType.DMA
    vm = pltpu.VMEM
    big = jax.ShapeDtypeStruct((lat, width), F32)
    vmem = pl.BlockSpec(memory_space=pltpu.VMEM)
    hbm = pl.BlockSpec(memory_space=pl.ANY)
    packed = (2 * rows, width // 2)
    return pl.pallas_call(
        functools.partial(kernel, Z, X, C, rows),
        out_shape=(
            big,
            big,
            jax.ShapeDtypeStruct((1, lat), F32),
            jax.ShapeDtypeStruct((8, 128), F32),
        ),
        in_specs=[vmem, vmem, vmem, hbm, hbm],
        out_specs=[vmem] * 4,
        scratch_shapes=[
            vm((lat, width), F32),
            vm((lat, width), F32),
            vm((lat, width), BF16),
            vm((lat, width), BF16),
            vm(packed, BF16),
            vm((Z,) + packed, BF16),
            vm((Z, pad, width), BF16),
            vm((Z, rows, lat), F32),
            vm((B, n, rows, lat), F32),
            vm((8, lat), F32),
            vm((n, 8, lat), F32),
            vm((1, lat), F32),
            vm((Z, pad, lat), BF16),
            vm((rows, width), F32),
            vm((Z,) + packed, BF16),
            vm((Z,) + packed, BF16),
            vm(packed, BF16),
            vm((Z,) + packed, BF16),
            vm((Z, pad, width), BF16),
            vm((Z, rows, lat), F32),
            vm((B, n, rows, lat), F32),
            vm((Z, pad, lat), BF16),
            vm((1, width), F32),
            vm((1, min(256, width)), F32),
            vm((Z, 8, 128), F32),
            vm((8, 128), F32),
            vm((n, 8, 128), F32),
            dma((2,)),
            dma((Z,)),
            dma((Z,)),
            dma((Z,)),
            dma((B, n)),
            dma((n,)),
            dma((n,)),
            dma((B, n)),
            dma((Z,)),
            dma((Z,)),
            dma((Z,)),
            dma((Z,)),
            dma((Z,)),
            dma((Z,)),
            dma((B, n)),
            dma((B, n)),
            dma((Z,)),
            dma((Z,)),
            dma((Z,)),
            dma((n,)),
            dma((n,)),
        ],
        compiler_params=pltpu.CompilerParams(
            collective_id=0, has_side_effects=True, vmem_limit_bytes=36 * 1024 * 1024
        ),
    )(inputs, dec_bias.reshape(1, -1), enc_bias.reshape(1, -1), enc_master, dec_master)


def per_device(
    Z, X, C,
    inputs, dec_bias, enc_master, enc_bias, dec_master, enc_m, enc_v, dec_m, dec_v, bias_m, bias_v,
):
    enc_grad, dec_grad, bias_grad, scalars = gradients(
        Z, X, C, inputs, dec_bias, enc_bias, enc_master, dec_master
    )
    clip_scale = scalars[0, 1]
    bias_grad = bias_grad.reshape(-1)
    enc_new, enc_m_new, enc_v_new = adam_update(enc_master, enc_m, enc_v, clip_scale * enc_grad)
    bias_new, bias_m_new, bias_v_new = adam_update(enc_bias, bias_m, bias_v, clip_scale * bias_grad)
    dec_new, dec_m_new, dec_v_new = adam_update(dec_master, dec_m, dec_v, clip_scale * dec_grad)
    return (
        enc_new,
        bias_new,
        dec_new,
        enc_m_new,
        enc_v_new,
        dec_m_new,
        dec_v_new,
        bias_m_new,
        bias_v_new,
        scalars[0, :1],
    )


def solution(mesh):
    matrix = P(("groups", "latent"), ("dp", "sub"))
    vector = P(("groups", "latent"))
    sizes = (mesh.shape["latent"], mesh.shape["dp"], mesh.shape["sub"])
    return jax.shard_map(
        functools.partial(per_device, *sizes),
        mesh=mesh,
        in_specs=(
            matrix, P(("groups", "dp", "sub")), matrix, vector, matrix,
            matrix, matrix, matrix, matrix, vector, vector,
        ),
        out_specs=(
            matrix, vector, matrix, matrix, matrix, matrix, matrix, vector, vector, P("groups"),
        ),
        check_vma=False,
    )
```

```python
import functools

import jax
import jax.numpy as jnp
from jax import lax
from jax.experimental import pallas as pl
from jax.experimental.pallas import tpu as pltpu
from jax.sharding import PartitionSpec as P

sparsity_coef = 5.0
clip_norm = 1.0
learn_rate = 0.01
beta_one = 0.9
beta_two = 0.999
adam_step = 100

MESH = pl.DeviceIdType.MESH
F32 = jnp.float32
BF16 = jnp.bfloat16
NT = (((1,), (1,)), ((), ()))
TN = (((0,), (0,)), ((), ()))


def adam_update(master, moment_one, moment_two, gradient):
    new_one = beta_one * moment_one + (1.0 - beta_one) * gradient
    new_two = beta_two * moment_two + (1.0 - beta_two) * gradient * gradient
    fix_one = 1.0 - beta_one**adam_step
    fix_two = 1.0 - beta_two**adam_step
    updated = master - learn_rate * (new_one / fix_one) / (jnp.sqrt(new_two / fix_two) + 1e-08)
    return (updated, new_one, new_two)


def when(cond):
    if isinstance(cond, bool):
        return (lambda f: f()) if cond else (lambda f: None)
    return pl.when(cond)


def steps(low, high, body, unroll):
    if unroll:
        for j in range(low, high):
            body(j)
    else:
        lax.fori_loop(low, high, lambda j, _: (body(j), 0)[1], 0)


def kernel(
    Z, X, C, rows, x_hbm, bias_hbm, enc_bias_hbm, enc_hbm, dec_hbm,
    enc_grad_ref, dec_grad_ref, bias_grad_ref, scalar_ref,
    x_ref, bias_ref, enc_bias_ref, enc_f, dec_f, enc_b, dec_b,
    cent_tx, cent_rx, cent, part_tx, part_rx, norm_tx, norm_rx, norm_row, act, recon_own,
    recon_tx, recon_rx, grad_tx, grad_rx, grad, back_tx, back_rx, pre, loss_acc, square_acc,
    one_rx, two_tx, two_rx,
    load_sem, cent_s, cent_r, part_s, part_r, norm_s, norm_r, act_s, act_r,
    recon_s, recon_r, grad_s, grad_r, back_s, back_r, pre_s, pre_r, one_s, one_r, two_s, two_r,
):
    n = X * C
    B = Z // n
    unroll = Z <= 4
    pad = cent.shape[1]
    width = cent.shape[2]
    half = width // 2
    lat = enc_f.shape[0]
    tokens = Z * rows
    z = lax.axis_index("latent")
    f = lax.axis_index("dp") * C + lax.axis_index("sub")

    def zdev(k):
        return {"latent": lax.rem(z + k, Z)}

    def fdev(q):
        return {"dp": lax.div(q, C), "sub": lax.rem(q, C)}

    def fpeer(k):
        return lax.rem(f + k, n)

    def remote(src, dst, s, r, dev):
        return pltpu.make_async_remote_copy(
            src_ref=src, dst_ref=dst, send_sem=s, recv_sem=r, device_id=dev, device_id_type=MESH
        )

    load_x = pltpu.make_async_copy(x_hbm, x_ref, load_sem.at[0])
    load_bias = pltpu.make_async_copy(bias_hbm, bias_ref, load_sem.at[1])
    load_dec = pltpu.make_async_copy(dec_hbm, dec_f, load_sem.at[2])
    load_enc = pltpu.make_async_copy(enc_hbm, enc_f, load_sem.at[3])
    load_enc_bias = pltpu.make_async_copy(enc_bias_hbm, enc_bias_ref, load_sem.at[4])
    for load in (load_x, load_bias, load_dec, load_enc, load_enc_bias):
        load.start()

    barrier = pltpu.get_barrier_semaphore()
    for k in range(1, Z):
        pl.semaphore_signal(barrier, inc=1, device_id=zdev(k), device_id_type=MESH)
    for k in range(1, n):
        pl.semaphore_signal(barrier, inc=1, device_id=fdev(fpeer(k)), device_id_type=MESH)

    def pack(ref, value):
        ref[...] = jnp.concatenate([value[:, :half], value[:, half:]], axis=0).astype(BF16)

    def unpack(ref):
        both = ref[...].astype(F32)
        return both[:rows], both[rows:]

    def place(ref, left, right):
        ref[:rows, :half] = left.astype(BF16)
        ref[:rows, half:] = right.astype(BF16)
        ref[rows:, :] = jnp.zeros((pad - rows, width), BF16)

    load_x.wait()
    load_bias.wait()
    x_own = x_ref[...].astype(F32)
    centered = x_own - bias_ref[...]
    pack(cent_tx, centered)
    place(cent.at[0], centered[:, :half], centered[:, half:])
    pl.semaphore_wait(barrier, Z - 1 + n - 1)

    fewer = jnp.minimum(z, Z - 1 - z)

    def nearest(t):
        paired = t <= 2 * fewer
        distance = jnp.where(paired, (t + 1) // 2, t - fewer)
        low = jnp.where(paired, t % 2, jnp.where(z > Z - 1 - z, 1, 0)) == 1
        return jnp.where(low, Z - distance, distance), low

    def neighbour_copies(tx, rx, s, r, action):
        @pl.when(z < Z - 1)
        def _():
            action(remote(tx, rx.at[Z - 1], s.at[0], r.at[Z - 1], {"latent": z + 1}))

        @pl.when(z > 0)
        def _():
            action(remote(tx, rx.at[1], s.at[Z], r.at[1], {"latent": z - 1}))

    def onward(rx, s, r, t, action):
        j, low = nearest(t)
        step = jnp.where(low, 1, -1)
        target = z + step

        @pl.when(jnp.logical_and(target >= 0, target < Z))
        def _():
            action(remote(rx.at[j], rx.at[j - step], s.at[j], r.at[j - step], {"latent": target}))

    def relay(rx, s, r, t):
        j, _ = nearest(t)
        remote(rx.at[j], rx.at[j], s.at[0], r.at[j], zdev(1)).wait_recv()
        onward(rx, s, r, t, start)
        return j

    def start(copy):
        copy.start()

    def wait_send(copy):
        copy.wait_send()

    def recon_copy(j):
        return remote(recon_tx.at[j], recon_rx.at[Z - j], recon_s.at[j], recon_r.at[Z - j], zdev(j))

    def norm_copy(k):
        return remote(norm_tx, norm_rx.at[f], norm_s.at[k], norm_r.at[f], fdev(fpeer(k)))

    def part_copy(tx, rx, s, r, j):
        return remote(tx.at[j], rx.at[j % B, f], s.at[j], r.at[j % B, f], fdev(j // B))

    def arrival(rx, s, r, jj, k):
        q = fpeer(k)
        return remote(rx.at[jj, q], rx.at[jj, q], s.at[0], r.at[jj, q], fdev(q))

    def share_copy(buf, s, r, j, k):
        return remote(buf.at[j], buf.at[j], s.at[j % B, k], r.at[j], fdev(fpeer(k)))

    def shared(buf, s, r, j):
        return remote(buf.at[j], buf.at[j], s.at[0, 0], r.at[j], fdev(fpeer(1)))

    neighbour_copies(cent_tx, cent_rx, cent_s, cent_r, start)

    load_dec.wait()
    dec = dec_f[...]
    dec_b[...] = dec.astype(BF16)
    column = jnp.sum(dec * dec, axis=1, keepdims=True)
    diag = lax.broadcasted_iota(jnp.int32, (lat, lat), 0) == lax.broadcasted_iota(
        jnp.int32, (lat, lat), 1
    )
    row = jnp.sum(jnp.where(diag, column, 0.0), axis=0, keepdims=True)
    norm_tx[...] = jnp.broadcast_to(row, norm_tx.shape)
    norm_rx[f] = jnp.broadcast_to(row, norm_tx.shape)
    for k in range(1, n):
        norm_copy(k).start()
    load_enc.wait()
    load_enc_bias.wait()
    enc_b[...] = enc_f[...].astype(BF16)
    loss_acc[...] = jnp.zeros_like(loss_acc)

    def sum_parts(rx, s, r, jj):
        for k in range(1, n):
            arrival(rx, s, r, jj, k).wait_recv()
        total = rx[jj, 0]
        for q in range(1, n):
            total = total + rx[jj, q]
        return total

    def send_part(value, tx, rx, s, r, j):
        owner = j // B

        @pl.when(f == owner)
        def _():
            rx[j % B, f] = value

        @pl.when(f != owner)
        def _():
            tx[j] = value
            part_copy(tx, rx, s, r, j).start()

    def set_shared(buf, s, r, j, value):
        buf[j, :rows, :] = value.astype(BF16)
        buf[j, rows:, :] = jnp.zeros((pad - rows, lat), BF16)
        for k in range(1, n):
            share_copy(buf, s, r, j, k).start()

    def block_of(t):
        return 0 if isinstance(t, int) and t == 0 else nearest(t)[0]

    def encode(t):
        j = block_of(t)

        @when(t > 0)
        def _():
            relay(cent_rx, cent_s, cent_r, t)
            place(cent.at[j], *unpack(cent_rx.at[j]))

        value = lax.dot_general(cent[j], enc_b[...], NT, preferred_element_type=F32)[:rows]
        send_part(value, part_tx, part_rx, part_s, part_r, j)

    def activate(t):
        j = block_of(t)

        @pl.when(f == j // B)
        def _():
            total = sum_parts(part_rx, part_s, part_r, j % B)
            active = jnp.maximum(total + enc_bias_ref[...], 0.0)
            set_shared(act, act_s, act_r, j, active)
            loss_acc[:, :lat] += sparsity_coef * jnp.sum(
                active * norm_row[...], axis=0, keepdims=True
            )

    def decode(t):
        j = block_of(t)

        @pl.when(f != j // B)
        def _():
            shared(act, act_s, act_r, j).wait_recv()

        value = jnp.dot(act[j], dec_b[...], preferred_element_type=F32)[:rows]

        @when(t == 0)
        def _():
            recon_own[...] = value

        @when(t > 0)
        def _():
            pack(recon_tx.at[j], value)
            recon_copy(j).start()

    def finish_norms():
        for k in range(1, n):
            q = fpeer(k)
            remote(norm_tx, norm_rx.at[q], norm_s.at[0], norm_r.at[q], fdev(q)).wait_recv()
        total = norm_rx[0]
        for q in range(1, n):
            total = total + norm_rx[q]
        norm_row[...] = jnp.sqrt(total[:1] + 1e-06)

    if unroll:
        encode(0)
        finish_norms()
        activate(0)
        encode(1)
        for s in range(2, Z + 2):
            if s < Z:
                encode(s)
            if s - 1 < Z:
                activate(s - 1)
            decode(s - 2)
    else:
        finish_norms()
        for stage in (encode, activate, decode):
            stage(0)
            steps(1, Z, stage, False)

    left = recon_own[:, :half]
    right = recon_own[:, half:]

    def add_rows(j, carry):
        remote(cent_tx, recon_rx.at[j], recon_s.at[0], recon_r.at[j], zdev(1)).wait_recv()
        one, two = unpack(recon_rx.at[j])
        return carry[0] + one, carry[1] + two

    if unroll:
        for j in range(1, Z):
            left, right = add_rows(j, (left, right))
    else:
        left, right = lax.fori_loop(1, Z, add_rows, (left, right))
    residual = jnp.concatenate([left, right], axis=1) + bias_ref[...] - x_own
    out_grad = residual * (2.0 / tokens)
    pack(grad_tx, out_grad)
    neighbour_copies(grad_tx, grad_rx, grad_s, grad_r, start)
    place(grad.at[0], out_grad[:, :half], out_grad[:, half:])
    error = jnp.sum(residual * residual, axis=0, keepdims=True)
    loss_acc[...] += error

    def back(t):
        j = block_of(t)

        @when(t > 0)
        def _():
            relay(grad_rx, grad_s, grad_r, t)
            place(grad.at[j], *unpack(grad_rx.at[j]))

        value = lax.dot_general(grad[j], dec_b[...], NT, preferred_element_type=F32)[:rows]
        send_part(value, back_tx, back_rx, back_s, back_r, j)

    def through(t):
        j = block_of(t)

        @pl.when(f == j // B)
        def _():
            total = sum_parts(back_rx, back_s, back_r, j % B)
            total = total + (sparsity_coef / tokens) * norm_row[...]
            value = jnp.where(act[j].astype(F32)[:rows] > 0.0, total, 0.0)
            set_shared(pre, pre_s, pre_r, j, value)

    if unroll:
        back(0)
        for s in range(1, Z + 1):
            if s < Z:
                back(s)
            through(s - 1)
    else:
        for stage in (back, through):
            stage(0)
            steps(1, Z, stage, False)

    act_all = act[...].reshape(Z * pad, lat)
    act_sum = jnp.sum(act_all.astype(F32), axis=0, keepdims=True)
    coef_row = (sparsity_coef / tokens) * act_sum / norm_row[...]
    coef = jnp.sum(jnp.where(diag, coef_row, 0.0), axis=1, keepdims=True)
    chunk = min(256, width)
    square_acc[...] = jnp.zeros_like(square_acc)
    for c in range(0, width, chunk):
        cols = slice(c, c + chunk)
        g = lax.dot_general(
            act_all, grad[:, :, cols].reshape(Z * pad, chunk), TN, preferred_element_type=F32
        )
        g = g + coef * dec_f[:, cols]
        dec_grad_ref[:, cols] = g
        square_acc[:, :chunk] += jnp.sum(g * g, axis=0, keepdims=True)

    def wait_pre(j):
        @pl.when(f != j // B)
        def _():
            shared(pre, pre_s, pre_r, j).wait_recv()

    steps(0, Z, wait_pre, unroll)
    pre_all = pre[...].reshape(Z * pad, lat)
    bias_grad = jnp.sum(pre_all.astype(F32), axis=0, keepdims=True)
    bias_grad_ref[...] = bias_grad
    for c in range(0, width, chunk):
        cols = slice(c, c + chunk)
        g = lax.dot_general(
            pre_all, cent[:, :, cols].reshape(Z * pad, chunk), TN, preferred_element_type=F32
        )
        enc_grad_ref[:, cols] = g
        square_acc[:, :chunk] += jnp.sum(g * g, axis=0, keepdims=True)

    first = jnp.where(f == 0, 1.0, 0.0)
    square = jnp.sum(square_acc[...], axis=1, keepdims=True) + first * jnp.sum(
        bias_grad * bias_grad, axis=1, keepdims=True
    )
    loss = jnp.sum(loss_acc[...], axis=1, keepdims=True)
    lane = lax.broadcasted_iota(jnp.int32, (8, 128), 1)
    own = jnp.where(lane == 0, loss, jnp.where(lane == 1, square, 0.0))

    one_rx[z] = own

    def one_copy(k):
        return remote(one_rx.at[z], one_rx.at[z], one_s.at[k], one_r.at[z], zdev(k))

    for k in range(1, Z):
        one_copy(k).start()
    for k in range(1, Z):
        src = lax.rem(z + k, Z)
        remote(one_rx.at[src], one_rx.at[src], one_s.at[0], one_r.at[src], zdev(k)).wait_recv()
    total = one_rx[0]
    for k in range(1, Z):
        total = total + one_rx[k]
    two_rx[f] = total

    def two_copy(k):
        return remote(two_rx.at[f], two_rx.at[f], two_s.at[k], two_r.at[f], fdev(fpeer(k)))

    for k in range(1, n):
        two_copy(k).start()
    for k in range(1, n):
        q = fpeer(k)
        remote(two_rx.at[q], two_rx.at[q], two_s.at[0], two_r.at[q], fdev(q)).wait_recv()
    total = two_rx[0]
    for q in range(1, n):
        total = total + two_rx[q]
    scale = jnp.minimum(1.0, clip_norm / jnp.sqrt(total + 1e-12))
    scalar_ref[...] = jnp.where(lane == 0, total * (1.0 / tokens), scale)

    for k in range(1, Z):
        one_copy(k).wait_send()
    for k in range(1, n):
        norm_copy(k).wait_send()
        two_copy(k).wait_send()

    neighbour_copies(cent_tx, cent_rx, cent_s, cent_r, wait_send)
    neighbour_copies(grad_tx, grad_rx, grad_s, grad_r, wait_send)

    def drain(j):
        @when(j > 0)
        def _():
            recon_copy(j).wait_send()
            onward(cent_rx, cent_s, cent_r, j, wait_send)
            onward(grad_rx, grad_s, grad_r, j, wait_send)

        @pl.when(f != j // B)
        def _():
            part_copy(part_tx, part_rx, part_s, part_r, j).wait_send()
            part_copy(back_tx, back_rx, back_s, back_r, j).wait_send()

        @pl.when(f == j // B)
        def _():
            for k in range(1, n):
                share_copy(act, act_s, act_r, j, k).wait_send()
                share_copy(pre, pre_s, pre_r, j, k).wait_send()

    steps(0, Z, drain, unroll)


def gradients(Z, X, C, inputs, dec_bias, enc_bias, enc_master, dec_master):
    rows, width = inputs.shape
    lat = enc_master.shape[0]
    n = X * C
    B = Z // n
    pad = -(-rows // 16) * 16
    dma = pltpu.SemaphoreType.DMA
    vm = pltpu.VMEM
    big = jax.ShapeDtypeStruct((lat, width), F32)
    vmem = pl.BlockSpec(memory_space=pltpu.VMEM)
    hbm = pl.BlockSpec(memory_space=pltpu.HBM)
    packed = (2 * rows, width // 2)
    return pl.pallas_call(
        functools.partial(kernel, Z, X, C, rows),
        out_shape=(
            big,
            big,
            jax.ShapeDtypeStruct((1, lat), F32),
            jax.ShapeDtypeStruct((8, 128), F32),
        ),
        in_specs=[hbm] * 5,
        out_specs=[vmem] * 4,
        scratch_shapes=[
            vm((rows, width), BF16),
            vm((1, width), F32),
            vm((1, lat), F32),
            vm((lat, width), F32),
            vm((lat, width), F32),
            vm((lat, width), BF16),
            vm((lat, width), BF16),
            vm(packed, BF16),
            vm((Z,) + packed, BF16),
            vm((Z, pad, width), BF16),
            vm((Z, rows, lat), F32),
            vm((B, n, rows, lat), F32),
            vm((8, lat), F32),
            vm((n, 8, lat), F32),
            vm((1, lat), F32),
            vm((Z, pad, lat), BF16),
            vm((rows, width), F32),
            vm((Z,) + packed, BF16),
            vm((Z,) + packed, BF16),
            vm(packed, BF16),
            vm((Z,) + packed, BF16),
            vm((Z, pad, width), BF16),
            vm((Z, rows, lat), F32),
            vm((B, n, rows, lat), F32),
            vm((Z, pad, lat), BF16),
            vm((1, width), F32),
            vm((1, min(256, width)), F32),
            vm((Z, 8, 128), F32),
            vm((8, 128), F32),
            vm((n, 8, 128), F32),
            dma((5,)),
            dma((Z + 1,)),
            dma((Z,)),
            dma((Z,)),
            dma((B, n)),
            dma((n,)),
            dma((n,)),
            dma((B, n)),
            dma((Z,)),
            dma((Z,)),
            dma((Z,)),
            dma((Z + 1,)),
            dma((Z,)),
            dma((Z,)),
            dma((B, n)),
            dma((B, n)),
            dma((Z,)),
            dma((Z,)),
            dma((Z,)),
            dma((n,)),
            dma((n,)),
        ],
        compiler_params=pltpu.CompilerParams(
            collective_id=0, has_side_effects=True, vmem_limit_bytes=60 * 1024 * 1024
        ),
    )(inputs, dec_bias.reshape(1, -1), enc_bias.reshape(1, -1), enc_master, dec_master)


def per_device(
    Z, X, C,
    inputs, dec_bias, enc_master, enc_bias, dec_master, enc_m, enc_v, dec_m, dec_v, bias_m, bias_v,
):
    enc_grad, dec_grad, bias_grad, scalars = gradients(
        Z, X, C, inputs, dec_bias, enc_bias, enc_master, dec_master
    )
    clip_scale = scalars[0, 1]
    bias_grad = bias_grad.reshape(-1)
    enc_new, enc_m_new, enc_v_new = adam_update(enc_master, enc_m, enc_v, clip_scale * enc_grad)
    bias_new, bias_m_new, bias_v_new = adam_update(enc_bias, bias_m, bias_v, clip_scale * bias_grad)
    dec_new, dec_m_new, dec_v_new = adam_update(dec_master, dec_m, dec_v, clip_scale * dec_grad)
    return (
        enc_new,
        bias_new,
        dec_new,
        enc_m_new,
        enc_v_new,
        dec_m_new,
        dec_v_new,
        bias_m_new,
        bias_v_new,
        scalars[0, :1],
    )


def solution(mesh):
    matrix = P(("groups", "latent"), ("dp", "sub"))
    vector = P(("groups", "latent"))
    sizes = (mesh.shape["latent"], mesh.shape["dp"], mesh.shape["sub"])
    return jax.shard_map(
        functools.partial(per_device, *sizes),
        mesh=mesh,
        in_specs=(
            matrix, P(("groups", "dp", "sub")), matrix, vector, matrix,
            matrix, matrix, matrix, matrix, vector, vector,
        ),
        out_specs=(
            matrix, vector, matrix, matrix, matrix, matrix, matrix, vector, vector, P("groups"),
        ),
        check_vma=False,
    )
```
